512 devices in a mesh: src: 64 (over x, y, core), rcv: 8 (over z).
Axes of the slice: x: 4, y: 8, z: 8, core: 2. Of those that a mesh axis runs over, the one named last changes fastest.
Arguments:
- spectra: bfloat16 [256, 8, 3, 4096], P('src', 'rcv'), may hold values from -200 to 200, as said below
- home: int32 [256], replicated, may hold values from 0 to 255, as said below
- lists: int32 [64, 128], P('src'), may hold values from -1 to 255, as said below
Outputs:
- correlations: float32 [64, 128, 8, 8, 128], P('src', None, None, 'rcv')
The draws below stay inside these ranges and needn't reach their ends.
Inputs may be any that keep to these rules, and one draw needn't show every extreme that they name: `spectra`: real parts in the first 2048 entries of the last dimension, imaginary parts in the last 2048. A permutation: block b is stored at position home[b]; position p lies on src index p // 4, in its slot p % 4. Each row lists distinct blocks followed by -1 entries, at least 64 blocks; no row lists more than 2 blocks stored on one src index, and some row lists 2 blocks from every src index.
All inputs are finite; a program needn't handle non-finite values.
Results may differ from the reference program's by a relative error of at most 0.007.
Values may be sent and summed in bfloat16 or wider, within the bound.
A program may use at most 64 MiB of HBM per device.

```python
import math
import jax
import jax.numpy as jnp
from jax import lax

F = 2048
LAGS = 128
W = 3
BS = 8
BAND = 32
CAP = 2
BLK_DEV = 4
NBLK = 256
LIST = 128
N_SRC = 64


def shared_homes(key):
    return jax.random.permutation(key, NBLK).astype(jnp.int32)


def draw_home(key, part):
    homes = shared_homes(key)
    return homes


def draw_lists(key, part):
    homes = shared_homes(key)
    key = jax.random.fold_in(key, 2)
    key_count, key_full, key_order, key_slot = jax.random.split(key, 4)
    owners = LIST // CAP
    cell_total = LIST
    counts = owners + jax.random.randint(key_count, (owners,), 0, owners + 1)
    full_row = jax.random.randint(key_full, (), 0, owners)
    counts = jnp.where(jnp.arange(owners) == full_row, cell_total, counts)
    order_scores = jax.random.randint(key_order, (owners, cell_total), 0, 1 << 20) * cell_total + jnp.arange(cell_total)[None, :]
    order = jnp.argsort(order_scores, axis=1).astype(jnp.int32)
    slot_scores = jax.random.randint(key_slot, (owners, owners, BLK_DEV), 0, 1 << 20) * BLK_DEV + jnp.arange(BLK_DEV)[None, None, :]
    slot_perm = jnp.argsort(slot_scores, axis=2).astype(jnp.int32)[..., :CAP]
    owner_dev = order // CAP
    cap_index = order % CAP
    row_ids = jnp.arange(owners)[:, None]
    local_slot = slot_perm[row_ids, owner_dev, cap_index]
    positions = owner_dev * BLK_DEV + local_slot
    inverse = jnp.argsort(homes).astype(jnp.int32)
    entries = inverse[positions]
    keep = jnp.arange(cell_total)[None, :] < counts[:, None]
    return jnp.where(keep, entries, -1).astype(jnp.int32)


def draw_spectra(key, part):
    key = jax.random.fold_in(key, 3)
    key_value, key_level = jax.random.split(key, 2)
    full_shape = (NBLK, BS, W, 2, F)
    values = jax.random.normal(key_value, full_shape, jnp.float32)
    level = jnp.exp(jax.random.uniform(key_level, (NBLK, BS, W, 1, F), jnp.float32, 0.0, math.log(10.0)))
    result = values * level
    return result.reshape(NBLK, BS, W, 2 * F).astype(jnp.bfloat16)


def setup_inputs(seed: int = 0) -> dict:
    splits = jax.random.split(jax.random.key(seed), 4)
    spectra = draw_spectra(jax.random.fold_in(splits[3], 71), 0)
    home = draw_home(jax.random.fold_in(splits[3], 71), 0)
    lists = draw_lists(jax.random.fold_in(splits[3], 71), 0)
    return dict(spectra=spectra, home=home, lists=lists)


def whiten(stored):
    values = stored.astype(jnp.float32)
    full_shape = values.shape
    freq_count = full_shape[-1] // 2
    halves = values.reshape(full_shape[:-1] + (2, freq_count // BAND, BAND))
    energy = lax.optimization_barrier(jnp.mean(halves[..., 0, :, :] * halves[..., 0, :, :] + halves[..., 1, :, :] * halves[..., 1, :, :], axis=-1, keepdims=True))
    scaled = halves * lax.rsqrt(energy + 1e-05)[..., None, :, :]
    return scaled.reshape(full_shape).astype(jnp.bfloat16)

def dft_table(freq_count, lag_count):
    freq_ids = jnp.arange(freq_count, dtype=jnp.int32)[:, None]
    lag_ids = jnp.arange(lag_count, dtype=jnp.int32)[None, :] - lag_count // 2
    turn_count = freq_ids * lag_ids % (2 * freq_count)
    angles = turn_count.astype(jnp.float32) * (math.pi / freq_count)
    factor = 1.0 / math.sqrt(freq_count)
    cosine = jnp.cos(angles) * factor
    sine_part = jnp.sin(angles) * factor
    top_half = jnp.concatenate([cosine, sine_part], axis=1)
    low_half = jnp.concatenate([-sine_part, cosine], axis=1)
    return jnp.concatenate([top_half, low_half], axis=0).astype(jnp.bfloat16)

def correlate(source_block, received, dft_matrix):
    freq_count = source_block.shape[-1] // 2
    lag_count = dft_matrix.shape[1] // 2
    src_real = source_block[..., :freq_count].astype(jnp.float32)[None, :, None]
    src_imag = source_block[..., freq_count:].astype(jnp.float32)[None, :, None]
    rcv_real = received[..., :freq_count].astype(jnp.float32)[:, None]
    rcv_imag = received[..., freq_count:].astype(jnp.float32)[:, None]
    cross_real = src_real * rcv_real + src_imag * rcv_imag
    cross_imag = src_imag * rcv_real - src_real * rcv_imag
    cross = jnp.concatenate([cross_real, cross_imag], axis=-1).astype(jnp.bfloat16)
    signal = jnp.dot(cross.reshape(-1, 2 * freq_count), dft_matrix, preferred_element_type=jnp.float32)
    signal = signal.reshape(cross.shape[:-1] + (2 * lag_count,))
    real_part = signal[..., :lag_count]
    imag_part = signal[..., lag_count:]
    energy = real_part * real_part + imag_part * imag_part
    floor_term = 0.1 * lax.optimization_barrier(jnp.mean(energy, axis=-1, keepdims=True)) + 1e-05
    inverse = lax.rsqrt(energy + floor_term)
    coherent = lax.optimization_barrier(jnp.mean(real_part * inverse, axis=3)) ** 2 + lax.optimization_barrier(jnp.mean(imag_part * inverse, axis=3)) ** 2
    linear = lax.optimization_barrier(jnp.mean(real_part, axis=3))
    return linear * coherent

def reference(spectra, home, lists):
    dft_matrix = dft_table(F, LAGS)
    list_len = lists.shape[1]

    def per_source(index):
        start = (index * BLK_DEV).astype(jnp.int32)
        source_block = whiten(lax.dynamic_index_in_dim(spectra, start, 0, keepdims=False))
        list_row = lists[index]
        is_valid = list_row >= 0
        position = home[jnp.where(is_valid, list_row, 0)].astype(jnp.int32)
        received = whiten(spectra[position])
        grouped = received.reshape((list_len // 4, 4) + received.shape[1:])

        def per_group(piece):
            return correlate(source_block, piece, dft_matrix)
        result = lax.map(per_group, grouped)
        result = result.reshape((list_len,) + result.shape[2:])
        return result * is_valid[:, None, None, None].astype(jnp.float32)
    return lax.map(per_source, jnp.arange(N_SRC, dtype=jnp.int32))
```

```python
import functools
import math

import jax
import jax.numpy as jnp
import numpy as np
from jax import lax
from jax.experimental import pallas as pl
from jax.experimental.pallas import tpu as pltpu
from jax.sharding import PartitionSpec as P

F = 2048
LAGS = 128
W = 3
BAND = 32
LIST = 128
X = 4
FT = 512
BF = jnp.bfloat16
F32 = jnp.float32
MESH = pl.DeviceIdType.MESH


def tables():
    freq = np.arange(F, dtype=np.int64)[:, None]
    lag = np.arange(LAGS, dtype=np.int64)[None, :] - LAGS // 2
    angle = ((freq * lag) % (2 * F)).astype(np.float64) * (math.pi / F)
    dft = np.concatenate([np.cos(angle), np.sin(angle)], axis=1) / math.sqrt(F)
    sel_s = np.zeros((16, W, 8, X, 16, W), np.float32)
    for r in range(8):
        for q in range(16):
            for w in range(W):
                sel_s[q, w, r, r // 2, q, w] = 1
    sel_r = np.zeros((4, W, 8, 4, W, 4), np.float32)
    for q in range(4):
        for w in range(W):
            sel_r[q, w, :, q, w, :] = 1
    block = np.zeros((8, 4, W, 4), np.float32) + np.arange(4)[None, None, None, :]
    lanes = np.arange(128)
    band = (lanes[:, None] // BAND == lanes[None, :] // BAND) / BAND
    return (
        dft.astype(np.float32).astype(BF),
        sel_s.reshape(16 * W * 8, X * 16 * W).astype(BF),
        sel_r.reshape(4 * W * 8, 4 * 4 * W),
        block.reshape(8, 4 * 4 * W),
        band.astype(BF),
    )


def exact_dot(a, b):
    hi = a.astype(BF)
    rest = a - hi.astype(F32)
    mid = rest.astype(BF)
    low = (rest - mid.astype(F32)).astype(BF)
    dot = functools.partial(jnp.dot, preferred_element_type=F32)
    return dot(hi, b) + dot(mid, b) + dot(low, b)


def kernel(
    Y, Z,
    spec_ref, home_ref, lists_ref, dft_hbm, sel_s_ref, sel_r_ref, block_ref, band_ref,
    out_ref,
    dft, rf, sf, rbuf, sbuf, gbuf, ubuf, vbuf, rg, tbuf, obuf, ibuf, of, osel,
    dft_sem, yss, yrs, qss, qrs, xss, xrs, gss, grs, zass, zars, zbss, zbrs, bxss, bxrs,
    oss, ors,
):
    HY, HZ = Y // 2, Z // 2
    src = lax.axis_index("src")
    z = lax.axis_index("rcv")
    c = lax.rem(src, 2)
    y = lax.rem(src // 2, Y)
    x = src // (2 * Y)

    def dev(xx, yy, cc, zz):
        return ((xx * Y + yy) * 2 + cc, zz)

    def mod(a, n):
        return lax.rem(a + n, n)

    def remote(a, b, ss, rs, device):
        return pltpu.make_async_remote_copy(
            src_ref=a, dst_ref=b, send_sem=ss, recv_sem=rs, device_id=device, device_id_type=MESH
        )

    barrier = pltpu.get_barrier_semaphore()
    peers = [dev(x, y, 1 - c, z)]
    if Y > 1:
        peers += [dev(x, mod(y + 1, Y), c, z), dev(x, mod(y - 1, Y), c, z)]
    peers += [dev(mod(x + d, X), y, c, z) for d in range(1, X)]
    peers += [dev(x, y, c, mod(z + d, Z)) for d in range(1, Z)]
    for peer in peers:
        pl.semaphore_signal(barrier, inc=1, device_id=peer, device_id_type=MESH)

    load_dft = pltpu.make_async_copy(dft_hbm, dft, dft_sem)
    load_dft.start()
    if Y < 8:
        ibuf[...] = jnp.zeros_like(ibuf)
        obuf[...] = jnp.zeros_like(obuf)

    pad = jnp.zeros((4, F), F32)
    spectra, energies = [], []
    for w in range(W):
        s = spec_ref[w].astype(F32)
        spectra.append(s)
        e = s[:, :F] * s[:, :F] + s[:, F:] * s[:, F:]
        e = jnp.concatenate([e, pad], axis=0)
        energies += [e[:, t * 128 : t * 128 + 128] for t in range(16)]
    mean = exact_dot(jnp.concatenate(energies, axis=0), band_ref[...])
    scale = lax.rsqrt(mean + 1e-05)
    for w in range(W):
        for t in range(16):
            k = scale[(w * 16 + t) * 8 : (w * 16 + t) * 8 + 4]
            for part in range(2):
                v = spectra[w][:, part * F + t * 128 : part * F + t * 128 + 128] * k
                q, lane = part * 2 + t // 8, (t % 8) * 128
                rf[pl.ds(q * 12 + w * 4, 4), pl.ds(lane, 128)] = v
                sf[pl.ds(t * 3 + w, 1), pl.ds(part * 128, 128)] = v[:1]
    rbuf[c, y] = rf[...].astype(BF)
    sbuf[z, x] = sf[...].astype(BF)

    sub = lax.broadcasted_iota(jnp.int32, (128, 128), 0)
    listed = lists_ref[...]
    home = home_ref[...].astype(F32)
    pos = jnp.zeros((1, 128), F32)
    for h in range(2):
        column = jnp.transpose(jnp.broadcast_to(home[h : h + 1], (128, 128)))
        hit = listed == sub + h * 128
        pos = pos + jnp.sum(jnp.where(hit, column, 0.0), axis=0, keepdims=True)
    pos = jnp.where(listed >= 0, pos, -1.0)
    pos = jnp.transpose(jnp.broadcast_to(pos, (128, 128)))
    lane = lax.broadcasted_iota(jnp.int32, (1, 128), 1)
    lane_c = (lane >> 4) & 1
    lane_n = (lane >> 1) & 7
    lane_y = (y + jnp.where((lane_n & 1) == 1, (lane_n + 1) >> 1, Y - (lane_n >> 1))) & (Y - 1)
    base = ((((lane >> 5) * Y + lane_y) * 2 + (lane & 1)) * 4).astype(F32)
    base = jnp.where(lane_n < Y, base, -100.0)
    has = [
        jnp.max(jnp.where(pos == base + b, 1.0, 0.0), axis=0, keepdims=True) > 0.5
        for b in range(4)
    ]
    first = jnp.where(has[0], 0.0, jnp.where(has[1], 1.0, jnp.where(has[2], 2.0, 3.0)))
    last = jnp.where(has[3], 3.0, jnp.where(has[2], 2.0, jnp.where(has[1], 1.0, 0.0)))
    pick = jnp.where(lane_c == 1, last, first)
    target = jnp.where((lane_c == 1) & (first == last), -50.0, base + pick)
    osel[...] = jnp.where(pos == target, 1.0, 0.0).astype(BF)
    gbuf[x] = jnp.broadcast_to(pick, (8, 128))

    pl.semaphore_wait(barrier, len(peers))

    started = []

    def start(copy):
        copy.start()
        started.append(copy)

    def x_peer(d):
        return dev(mod(x + d, X), y, c, z)

    def y_copy(way, d, h):
        at = mod(y - d, Y) if way == 0 else mod(y + d, Y)
        to = mod(y + 1, Y) if way == 0 else mod(y - 1, Y)
        ref = rbuf.at[c, at, :, pl.ds(h * 512, 512)]
        return remote(ref, ref, yss.at[way, d, h], yrs.at[way, d, h], dev(x, to, c, z))

    def y_pieces(way, d):
        return (0, 1) if d + 1 < HY else ((way,) if d + 1 == HY else ())

    def q_copy(rel, h):
        ref = rbuf.at[c, mod(y + rel, Y), :, pl.ds(h * 512, 512)]
        return remote(ref, ref, qss.at[rel, h], qrs.at[rel, h], dev(x, y, 1 - c, z))

    def q_arrival(rel, h):
        ref = rbuf.at[1 - c, mod(y + rel, Y), :, pl.ds(h * 512, 512)]
        return remote(ref, ref, qss.at[rel, h], qrs.at[rel, h], dev(x, y, 1 - c, z))

    def xa_copy(d):
        ref = sbuf.at[z, x, :, pl.ds(0, 128)]
        return remote(ref, ref, xss.at[d - 1], xrs.at[d - 1], x_peer(d))

    def xa_arrival(d):
        ref = sbuf.at[z, mod(x - d, X), :, pl.ds(0, 128)]
        return remote(ref, ref, xss.at[d - 1], xrs.at[d - 1], x_peer(d))

    def g_copy(d):
        return remote(gbuf.at[x], gbuf.at[x], gss.at[d - 1], grs.at[d - 1], x_peer(d))

    def g_arrival(d):
        ref = gbuf.at[mod(x - d, X)]
        return remote(ref, ref, gss.at[d - 1], grs.at[d - 1], x_peer(d))

    def za_copy(way, d, arrival=False):
        to = mod(z + 1, Z) if way == 0 else mod(z - 1, Z)
        e = d + 1 if arrival else d
        at = mod(z - e, Z) if way == 0 else mod(z + e, Z)
        if d + 1 < HZ:
            ref = sbuf.at[at, :, :, pl.ds(0, 128)]
        else:
            ref = sbuf.at[at, pl.ds(way * 2, 2), :, pl.ds(0, 128)]
        return remote(ref, ref, zass.at[way, d], zars.at[way, d], dev(x, y, c, to))

    def y_arrival(way, d, h):
        e = d + 1
        at = mod(y - e, Y) if way == 0 else mod(y + e, Y)
        ref = rbuf.at[c, at, :, pl.ds(h * 512, 512)]
        return remote(ref, ref, yss.at[way, d, h], yrs.at[way, d, h], dev(x, y, 1 - c, z))

    def zb_copy(d):
        ref = sbuf.at[z, x, :, pl.ds(128, 128)]
        return remote(ref, ref, zbss.at[d - 1], zbrs.at[d - 1], dev(x, y, c, mod(z + d, Z)))

    def zb_arrival(d):
        ref = sbuf.at[mod(z - d, Z), x, :, pl.ds(128, 128)]
        return remote(ref, ref, zbss.at[d - 1], zbrs.at[d - 1], dev(x, y, c, mod(z + d, Z)))

    def bx_copy(d, rel):
        ref = sbuf.at[mod(z + rel, Z), x, :, pl.ds(128, 128)]
        return remote(ref, ref, bxss.at[d - 1, rel], bxrs.at[d - 1, rel], x_peer(d))

    def bx_arrival(d, rel):
        ref = sbuf.at[mod(z + rel, Z), mod(x - d, X), :, pl.ds(128, 128)]
        return remote(ref, ref, bxss.at[d - 1, rel], bxrs.at[d - 1, rel], x_peer(d))

    M = 2 * Z

    def o_copy(d, n):
        rows = pl.ds(pl.multiple_of(n * M, M), M)
        to = mod(x + d, X)
        return remote(
            obuf.at[to, :, rows], ibuf.at[x, :, rows], oss.at[d - 1, n], ors.at[d - 1, n], x_peer(d)
        )

    def o_arrival(d, n):
        rows = pl.ds(pl.multiple_of(n * M, M), M)
        ref = ibuf.at[mod(x - d, X), :, rows]
        return remote(ref, ref, oss.at[d - 1, n], ors.at[d - 1, n], x_peer(d))

    for d in range(1, X):
        start(xa_copy(d))
    for d in range(1, Z):
        start(zb_copy(d))
    for way in range(2):
        for h in y_pieces(way, 0):
            start(y_copy(way, 0, h))
    for d in range(1, X):
        start(g_copy(d))
    for d in range(1, X):
        start(bx_copy(d, 0))
    for h in range(2):
        start(q_copy(0, h))
    for d in range(1, X):
        xa_arrival(d).wait_recv()
    if HZ:
        for way in range(2):
            start(za_copy(way, 0))
    for d in range(1, X):
        g_arrival(d).wait_recv()

    def z_step(d):
        for way in range(2):
            if d <= HZ:
                za_copy(way, d - 1, arrival=True).wait_recv()
                if d < HZ:
                    start(za_copy(way, d))
        for e in sorted({d, Z - d}):
            if d <= HZ:
                zb_arrival(e).wait_recv()
                for k in range(1, X):
                    start(bx_copy(k, Z - e))

    def y_step(d):
        for way in range(2):
            for h in y_pieces(way, d - 1):
                y_arrival(way, d - 1, h).wait_recv()
                if h in y_pieces(way, d):
                    start(y_copy(way, d, h))
                rel = Y - d if way == 0 else d
                start(q_copy(rel, h))

    def assemble(rel):
        at = mod(z + rel, Z)
        for d in range(1, X):
            bx_arrival(d, rel).wait_recv()
        rows = jnp.dot(
            sel_s_ref[...], sbuf[at].reshape(X * 48, 256), preferred_element_type=F32
        )
        for q in range(16):
            for w in range(W):
                v = rows[(q * W + w) * 8 : (q * W + w) * 8 + 8]
                re, im = v[:, :128], v[:, 128:]
                ubuf[at, w, :, pl.ds(q * 128, 128)] = jnp.concatenate([re, im], axis=0).astype(BF)
                vbuf[at, w, :, pl.ds(q * 128, 128)] = jnp.concatenate([im, -re], axis=0).astype(BF)

    for d in range(1, max(HY, HZ + 1)):
        if d <= HZ:
            z_step(d)
        if d < HY:
            y_step(d)
        for rel in sorted({d - 1, (Z - d + 1) % Z}):
            assemble(rel)
    if HZ:
        assemble(HZ)
    elif HY <= 1:
        assemble(0)
    load_dft.wait()

    g_rows = lax.broadcasted_iota(jnp.int32, (8, 128), 0)
    g_lanes = lax.broadcasted_iota(jnp.int32, (8, 128), 1)
    picks = gbuf[0]
    for s in range(1, X):
        picks = jnp.where((g_rows >> 1) == s, gbuf[s], picks)

    @pl.loop(0, Y)
    def _(n):
        rel = jnp.where(lax.rem(n, 2) == 1, (n + 1) // 2, lax.rem(Y - n // 2, Y))
        at = mod(y + rel, Y)
        if HY:

            @pl.when(n == max(Y - 3, 0))
            def _():
                for way in range(2):
                    y_arrival(way, HY - 1, way).wait_recv()
                    q_copy(HY, way).start()

        for h in range(2):
            q_arrival(rel, h).wait_recv()

        for core in range(2):
            mark = x * 32 + (g_rows & 1) * 16 + n * 2 + core
            column = jnp.sum(jnp.where(g_lanes == mark, picks, 0.0), axis=1, keepdims=True)
            sel = jnp.where(block_ref[...] == column, 1.0, 0.0)
            sel = (jnp.concatenate([sel] * 12, axis=0) * sel_r_ref[...]).astype(BF)
            rows = jnp.dot(sel, rbuf[core, at], preferred_element_type=F32)
            for q in range(4):
                for w in range(W):
                    v = rows[(q * W + w) * 8 : (q * W + w) * 8 + 8]
                    rg[core, w, q // 2, :, pl.ds((q % 2) * 1024, 1024)] = jnp.concatenate(
                        [v, v], axis=0
                    ).astype(BF)

        signal = None
        for f in range(0, F, FT):
            fs = pl.ds(f, FT)
            rows = []
            for w in range(W):
                for core in range(2):
                    rr, ri = rg[core, w, 0, :, fs], rg[core, w, 1, :, fs]
                    for i in range(Z):
                        rows.append(ubuf[i, w, :, fs] * rr + vbuf[i, w, :, fs] * ri)
            part = jnp.dot(jnp.concatenate(rows, axis=0), dft[fs, :], preferred_element_type=F32)
            signal = part if signal is None else signal + part
        signal = signal.reshape(W, M, 2, 8, 256)
        real = signal[:, :, 0, :, :128] - signal[:, :, 1, :, 128:]
        imag = signal[:, :, 0, :, 128:] + signal[:, :, 1, :, :128]
        energy = real * real + imag * imag
        inverse = lax.rsqrt(energy + (0.1 * jnp.mean(energy, axis=-1, keepdims=True) + 1e-05))
        pr, pi = real * inverse, imag * inverse
        third = 1.0 / 3.0
        mr = (pr[0] + pr[1] + pr[2]) * third
        mi = (pi[0] + pi[1] + pi[2]) * third
        tbuf[...] = ((real[0] + real[1] + real[2]) * third) * (mr * mr + mi * mi)
        at_rows = pl.ds(pl.multiple_of(n * M, M), M)
        for s in range(X):
            for k in range(2):
                obuf[s, k, at_rows, :] = tbuf[:, 2 * s + k, :].astype(BF)
        for d in range(1, X):
            o_copy(d, n).start()

    for copy in started:
        copy.wait_send()
    if HY:
        for way in range(2):
            q_copy(HY, way).wait_send()
    ibuf[x] = obuf[x]
    for d in range(1, X):
        for n in range(Y):
            o_copy(d, n).wait_send()
            o_arrival(d, n).wait_recv()
    of[...] = ibuf[...].astype(F32).reshape(128 * Z, 128)
    for i in range(Z):
        rows = of[pl.ds(i, 128, stride=Z), :].astype(BF)
        out_ref[:, i, :] = jnp.dot(osel[...], rows, preferred_element_type=F32)


def body(spectra, home, lists, Y, Z):
    dft, sel_s, sel_r, block, band = (jnp.asarray(t) for t in tables())
    vmem = pl.BlockSpec(memory_space=pltpu.VMEM)
    dma = pltpu.SemaphoreType.DMA
    HY, HZ = max(Y // 2, 1), max(Z // 2, 1)
    out = pl.pallas_call(
        functools.partial(kernel, Y, Z),
        out_shape=jax.ShapeDtypeStruct((LIST, Z, LAGS), F32),
        in_specs=[vmem] * 3 + [pl.BlockSpec(memory_space=pl.ANY)] + [vmem] * 4,
        out_specs=vmem,
        scratch_shapes=[
            pltpu.VMEM((F, 2 * LAGS), BF),
            pltpu.VMEM((48, 1024), F32),
            pltpu.VMEM((48, 256), F32),
            pltpu.VMEM((2, Y, 48, 1024), BF),
            pltpu.VMEM((Z, X, 48, 256), BF),
            pltpu.VMEM((X, 8, 128), F32),
            pltpu.VMEM((Z, W, 16, F), BF),
            pltpu.VMEM((Z, W, 16, F), BF),
            pltpu.VMEM((2, W, 2, 16, F), BF),
            pltpu.VMEM((2 * Z, 8, 128), F32),
            pltpu.VMEM((X, 2, 16 * Z, 128), BF),
            pltpu.VMEM((X, 2, 16 * Z, 128), BF),
            pltpu.VMEM((128 * Z, 128), F32),
            pltpu.VMEM((128, 128), BF),
            dma,
            dma((2, HY, 2)), dma((2, HY, 2)),
            dma((Y, 2)), dma((Y, 2)),
            dma((X - 1,)), dma((X - 1,)),
            dma((X - 1,)), dma((X - 1,)),
            dma((2, HZ)), dma((2, HZ)),
            dma((max(Z - 1, 1),)), dma((max(Z - 1, 1),)),
            dma((X - 1, Z)), dma((X - 1, Z)),
            dma((X - 1, Y)), dma((X - 1, Y)),
        ],
        compiler_params=pltpu.CompilerParams(
            collective_id=0, has_side_effects=True, vmem_limit_bytes=48 * 2**20
        ),
        cost_estimate=pl.CostEstimate(
            flops=6_500_000_000, bytes_accessed=4_000_000, transcendentals=400_000
        ),
    )(spectra.transpose(1, 2, 0, 3)[0], home.reshape(2, 128), lists, dft, sel_s, sel_r, block, band)
    return out[None, :, :, None, :]


def solution(mesh):
    Y = mesh.shape["src"] // (2 * X)
    Z = mesh.shape["rcv"]
    return jax.shard_map(
        functools.partial(body, Y=Y, Z=Z),
        mesh=mesh,
        in_specs=(P("src", "rcv", None, None), P(), P("src", None)),
        out_specs=P("src", None, None, "rcv", None),
        check_vma=False,
    )
```

```python
import functools
import math

import jax
import jax.numpy as jnp
import numpy as np
from jax import lax
from jax.experimental import pallas as pl
from jax.experimental.pallas import tpu as pltpu
from jax.sharding import PartitionSpec as P

F = 2048
LAGS = 128
W = 3
BAND = 32
LIST = 128
X = 4
FT = 512
BF = jnp.bfloat16
F32 = jnp.float32
MESH = pl.DeviceIdType.MESH


def tables():
    freq = np.arange(F, dtype=np.int64)[:, None]
    lag = np.arange(LAGS, dtype=np.int64)[None, :] - LAGS // 2
    angle = ((freq * lag) % (2 * F)).astype(np.float64) * (math.pi / F)
    dft = np.concatenate([np.cos(angle), np.sin(angle)], axis=1) / math.sqrt(F)
    sel_s = np.zeros((16, W, 8, X, 16, W), np.float32)
    for r in range(8):
        for q in range(16):
            for w in range(W):
                sel_s[q, w, r, r // 2, q, w] = 1
    sel_r = np.zeros((4, W, 8, 4, W, 4), np.float32)
    for q in range(4):
        for w in range(W):
            sel_r[q, w, :, q, w, :] = 1
    block = np.zeros((8, 4, W, 4), np.float32) + np.arange(4)[None, None, None, :]
    lanes = np.arange(128)
    band = (lanes[:, None] // BAND == lanes[None, :] // BAND) / BAND
    return (
        dft.astype(np.float32).astype(BF),
        sel_s.reshape(16 * W * 8, X * 16 * W).astype(BF),
        sel_r.reshape(4 * W * 8, 4 * 4 * W),
        block.reshape(8, 4 * 4 * W),
        band.astype(BF),
    )


def exact_dot(a, b):
    hi = a.astype(BF)
    rest = a - hi.astype(F32)
    mid = rest.astype(BF)
    low = (rest - mid.astype(F32)).astype(BF)
    dot = functools.partial(jnp.dot, preferred_element_type=F32)
    return dot(hi, b) + dot(mid, b) + dot(low, b)


def kernel(
    Y, Z,
    spec_hbm, home_hbm, lists_hbm, dft_hbm, sel_s_hbm, sel_r_hbm, block_hbm, band_hbm,
    out_ref,
    spec_ref, home_ref, lists_ref, dft, sel_s_ref, sel_r_ref, block_ref, band_ref,
    rf, sf, rbuf, sbuf, gbuf, ubuf, vbuf, rg, tbuf, obuf, ibuf, of, osel,
    in_sem, yss, yrs, qss, qrs, gss, grs, nss, nrs, zss, zrs, xss, xrs, oss, ors,
):
    HY, HZ = Y // 2, Z // 2
    src = lax.axis_index("src")
    z = lax.axis_index("rcv")
    c = lax.rem(src, 2)
    y = lax.rem(src // 2, Y)
    x = src // (2 * Y)
    order = [0]
    for d in range(1, HZ + 1):
        order += sorted({d, Z - d})

    def dev(xx, yy, cc, zz):
        return ((xx * Y + yy) * 2 + cc, zz)

    def mod(a, n):
        return lax.rem(a + n, n)

    def remote(a, b, ss, rs, device):
        return pltpu.make_async_remote_copy(
            src_ref=a, dst_ref=b, send_sem=ss, recv_sem=rs, device_id=device, device_id_type=MESH
        )

    barrier = pltpu.get_barrier_semaphore()
    peers = [dev(x, y, 1 - c, z)]
    peers += [dev(x, mod(y + 1, Y), c, z), dev(x, mod(y - 1, Y), c, z)]
    peers += [dev(mod(x + d, X), y, c, z) for d in range(1, X)]
    peers += [dev(x, y, c, mod(z + d, Z)) for d in range(1, Z)]
    for peer in peers:
        pl.semaphore_signal(barrier, inc=1, device_id=peer, device_id_type=MESH)

    loads = [
        pltpu.make_async_copy(a, b, in_sem.at[k])
        for k, (a, b) in enumerate((
            (spec_hbm, spec_ref), (band_hbm, band_ref), (home_hbm, home_ref),
            (lists_hbm, lists_ref), (sel_s_hbm, sel_s_ref), (sel_r_hbm, sel_r_ref),
            (block_hbm, block_ref), (dft_hbm, dft),
        ))
    ]
    for load in loads:
        load.start()
    if Y < 8:
        ibuf[...] = jnp.zeros_like(ibuf)
        obuf[...] = jnp.zeros_like(obuf)
    loads[0].wait()
    loads[1].wait()

    pad = jnp.zeros((4, F), F32)
    spectra, energies = [], []
    for w in range(W):
        s = spec_ref[w].astype(F32)
        spectra.append(s)
        e = s[:, :F] * s[:, :F] + s[:, F:] * s[:, F:]
        e = jnp.concatenate([e, pad], axis=0)
        energies += [e[:, t * 128 : t * 128 + 128] for t in range(16)]
    mean = exact_dot(jnp.concatenate(energies, axis=0), band_ref[...])
    scale = lax.rsqrt(mean + 1e-05)
    for w in range(W):
        for t in range(16):
            k = scale[(w * 16 + t) * 8 : (w * 16 + t) * 8 + 4]
            for part in range(2):
                v = spectra[w][:, part * F + t * 128 : part * F + t * 128 + 128] * k
                q, lane = part * 2 + t // 8, (t % 8) * 128
                rf[pl.ds(q * 12 + w * 4, 4), pl.ds(lane, 128)] = v
                sf[part, pl.ds(t * 3 + w, 1), :] = v[:1]
    whitened = rf[...].astype(BF)
    for h in range(2):
        rbuf[c, y, h] = whitened[:, h * 512 : h * 512 + 512]
    sbuf[z, x] = sf[...].astype(BF)

    pl.semaphore_wait(barrier, len(peers))

    started = []

    def start(copy):
        copy.start()
        started.append(copy)

    def x_peer(d):
        return dev(mod(x + d, X), y, c, z)

    def y_copy(way, d, h, arrival=False):
        e = d + 1 if arrival else d
        at = mod(y - e, Y) if way == 0 else mod(y + e, Y)
        to = mod(y + 1, Y) if way == 0 else mod(y - 1, Y)
        ref = rbuf.at[c, at, h]
        return remote(ref, ref, yss.at[way, d, h], yrs.at[way, d, h], dev(x, to, c, z))

    def y_pieces(way, d):
        return (0, 1) if d + 1 < HY else ((way,) if d + 1 == HY else ())

    def q_copy(rel, h, core):
        ref = rbuf.at[core, mod(y + rel, Y), h]
        return remote(ref, ref, qss.at[rel, h], qrs.at[rel, h], dev(x, y, 1 - c, z))

    def g_copy(d, origin):
        ref = gbuf.at[origin]
        return remote(ref, ref, gss.at[d - 1], grs.at[d - 1], x_peer(d))

    def z_copy(d, origin):
        ref = sbuf.at[origin, x]
        return remote(ref, ref, zss.at[d - 1], zrs.at[d - 1], dev(x, y, c, mod(z + d, Z)))

    def near_copy(way, origin):
        to = mod(z + 1, Z) if way == 0 else mod(z - 1, Z)
        ref = sbuf.at[origin]
        return remote(ref, ref, nss.at[way], nrs.at[way], dev(x, y, c, to))

    def x_copy(d, rel, origin):
        ref = sbuf.at[mod(z + rel, Z), origin]
        return remote(ref, ref, xss.at[d - 1, rel], xrs.at[d - 1, rel], x_peer(d))

    M = 2 * Z

    def o_copy(d, t, arrival=False):
        rows = pl.ds(pl.multiple_of(t * M, M), M)
        a = ibuf.at[mod(x - d, X), :, rows] if arrival else obuf.at[mod(x + d, X), :, rows]
        b = ibuf.at[mod(x - d, X) if arrival else x, :, rows]
        return remote(a, b, oss.at[d - 1, t], ors.at[d - 1, t], x_peer(d))

    near = (1, Z - 1) if Z > 2 else ()
    far = [d for d in order[1:] if d not in near]
    for d in far:
        start(z_copy(d, z))
    for d in range(1, X):
        start(x_copy(d, 0, x))
    for way in range(2):
        for h in y_pieces(way, 0):
            start(y_copy(way, 0, h))
    for h in range(2):
        start(q_copy(0, h, c))

    for load in loads[2:]:
        load.wait()
    sub = lax.broadcasted_iota(jnp.int32, (128, 128), 0)
    listed = lists_ref[...]
    home = home_ref[...].astype(F32)
    pos = jnp.zeros((1, 128), F32)
    for h in range(2):
        column = jnp.transpose(jnp.broadcast_to(home[h : h + 1], (128, 128)))
        hit = listed == sub + h * 128
        pos = pos + jnp.sum(jnp.where(hit, column, 0.0), axis=0, keepdims=True)
    pos = jnp.where(listed >= 0, pos, -1.0)
    pos = jnp.transpose(jnp.broadcast_to(pos, (128, 128)))
    lane = lax.broadcasted_iota(jnp.int32, (1, 128), 1)
    lane_c = (lane >> 4) & 1
    lane_n = (lane >> 1) & 7
    lane_y = (y + jnp.where((lane_n & 1) == 1, (lane_n + 1) >> 1, Y - (lane_n >> 1))) & (Y - 1)
    base = ((((lane >> 5) * Y + lane_y) * 2 + (lane & 1)) * 4).astype(F32)
    base = jnp.where(lane_n < Y, base, -100.0)
    has = [
        jnp.max(jnp.where(pos == base + b, 1.0, 0.0), axis=0, keepdims=True) > 0.5
        for b in range(4)
    ]
    first = jnp.where(has[0], 0.0, jnp.where(has[1], 1.0, jnp.where(has[2], 2.0, 3.0)))
    last = jnp.where(has[3], 3.0, jnp.where(has[2], 2.0, jnp.where(has[1], 1.0, 0.0)))
    pick = jnp.where(lane_c == 1, last, first)
    target = jnp.where((lane_c == 1) & (first == last), -50.0, base + pick)
    osel[...] = jnp.where(pos == target, 1.0, 0.0).astype(BF)
    gbuf[x] = jnp.broadcast_to(pick, (8, 128))

    for d in range(1, X):
        start(g_copy(d, x))

    def z_step(rel):
        z_copy(Z - rel, mod(z + rel, Z)).wait_recv()
        for k in range(1, X):
            start(x_copy(k, rel, x))

    def y_step(d, send):
        for way in range(2):
            for h in y_pieces(way, d - 1):
                y_copy(way, d - 1, h, arrival=True).wait_recv()
                if h in y_pieces(way, d):
                    send(y_copy(way, d, h))
                send(q_copy(Y - d if way == 0 else d, h, c))

    def assemble(k):
        rel = order[k]
        at = mod(z + rel, Z)
        if rel in near:
            near_copy(near.index(rel) ^ 1, at).wait_recv()
        elif rel:
            for d in range(1, X):
                x_copy(d, rel, mod(x - d, X)).wait_recv()
        parts = sbuf[at]
        parts = jnp.concatenate(
            [parts[:, 0].reshape(X * 48, 128), parts[:, 1].reshape(X * 48, 128)], axis=1
        )
        rows = jnp.dot(sel_s_ref[...], parts, preferred_element_type=F32)
        for q in range(16):
            for w in range(W):
                v = rows[(q * W + w) * 8 : (q * W + w) * 8 + 8]
                re, im = v[:, :128], v[:, 128:]
                ubuf[k, w, :, pl.ds(q * 128, 128)] = jnp.concatenate([re, im], axis=0).astype(BF)
                vbuf[k, w, :, pl.ds(q * 128, 128)] = jnp.concatenate([im, -re], axis=0).astype(BF)

    NM = HY
    for d in range(1, X):
        x_copy(d, 0, mod(x - d, X)).wait_recv()
    if near:
        for way in range(2):
            start(near_copy(way, z))
    if HY > 1:
        y_step(1, start)
    assemble(0)
    if HY > 2:
        y_step(2, start)
    for rel in far:
        z_step(rel)
    for k in range(1, HZ):
        assemble(k)
    for d in range(1, X):
        g_copy(d, mod(x - d, X)).wait_recv()

    g_rows = lax.broadcasted_iota(jnp.int32, (8, 128), 0)
    g_lanes = lax.broadcasted_iota(jnp.int32, (8, 128), 1)
    picks = gbuf[0]
    for s in range(1, X):
        picks = jnp.where((g_rows >> 1) == s, gbuf[s], picks)

    def begin(copy):
        copy.start()

    second = NM - 1 if NM > 1 else 1

    @pl.loop(0, 2 * NM)
    def _(t):
        half = jnp.where(t < NM - 1, 0, jnp.where(t < 2 * NM - 2, 1, t - (2 * NM - 2)))
        m = jnp.where(t < NM - 1, t, jnp.where(t < 2 * NM - 2, t - (NM - 1), NM - 1))
        if HY > 3:

            @pl.when(t == 1)
            def _():
                y_step(3, begin)

        @pl.when(t == max(2 * NM - 5, 0))
        def _():
            y_step(HY, begin)

        @pl.when(t == second)
        def _():
            for k in range(HZ, Z):
                assemble(k)

        @pl.when(half == 0)
        def _():
            for u in range(2):
                n = 2 * m + u
                rel = jnp.where(u == 1, m + 1, lax.rem(Y - m, Y))
                at = mod(y + rel, Y)
                for h in range(2):
                    q_copy(rel, h, 1 - c).wait_recv()
                for core in range(2):
                    mark = x * 32 + (g_rows & 1) * 16 + n * 2 + core
                    column = jnp.sum(jnp.where(g_lanes == mark, picks, 0.0), axis=1, keepdims=True)
                    sel = jnp.where(block_ref[...] == column, 1.0, 0.0)
                    sel = (jnp.concatenate([sel] * 12, axis=0) * sel_r_ref[...]).astype(BF)
                    for h in range(2):
                        rows = jnp.dot(sel, rbuf[core, at, h], preferred_element_type=F32)
                        for q in range(4):
                            for w in range(W):
                                v = rows[(q * W + w) * 8 : (q * W + w) * 8 + 8]
                                rg[2 * n + core, w, q // 2, :, pl.ds((q % 2) * 1024 + h * 512, 512)] = (
                                    jnp.concatenate([v, v], axis=0).astype(BF)
                                )

        signal = None
        for f in range(0, F, FT):
            fs = pl.ds(f, FT)
            rows = []
            for w in range(W):
                for u in range(4):
                    rr, ri = rg[4 * m + u, w, 0, :, fs], rg[4 * m + u, w, 1, :, fs]
                    for k in range(HZ):
                        i = half * HZ + k
                        rows.append(ubuf[i, w, :, fs] * rr + vbuf[i, w, :, fs] * ri)
            part = jnp.dot(jnp.concatenate(rows, axis=0), dft[fs, :], preferred_element_type=F32)
            signal = part if signal is None else signal + part
        signal = signal.reshape(W, M, 2, 8, 256)
        real = signal[:, :, 0, :, :128] - signal[:, :, 1, :, 128:]
        imag = signal[:, :, 0, :, 128:] + signal[:, :, 1, :, :128]
        energy = real * real + imag * imag
        inverse = lax.rsqrt(energy + (0.1 * jnp.mean(energy, axis=-1, keepdims=True) + 1e-05))
        pr, pi = real * inverse, imag * inverse
        third = 1.0 / 3.0
        mr = (pr[0] + pr[1] + pr[2]) * third
        mi = (pi[0] + pi[1] + pi[2]) * third
        tbuf[...] = ((real[0] + real[1] + real[2]) * third) * (mr * mr + mi * mi)
        slot = m * 2 + half
        at_rows = pl.ds(pl.multiple_of(slot * M, M), M)
        for s in range(X):
            for k in range(2):
                obuf[s, k, at_rows, :] = tbuf[:, 2 * s + k, :].astype(BF)
        for d in range(1, X):
            o_copy(d, slot).start()

    for copy in started:
        copy.wait_send()
    for d in sorted({HY, 3} if HY > 3 else {HY}):
        for way in range(2):
            for h in y_pieces(way, d - 1):
                if h in y_pieces(way, d):
                    y_copy(way, d, h).wait_send()
                q_copy(Y - d if way == 0 else d, h, c).wait_send()
    ibuf[x] = obuf[x]
    for d in range(1, X):
        for t in range(2 * NM):
            o_copy(d, t).wait_send()
            o_copy(d, t, arrival=True).wait_recv()
    of[...] = ibuf[...].astype(F32).reshape(X * 2 * 8 * 2 * Z, 128)
    for k in range(Z):
        rows = []
        for block in range(X * 2 * 4):
            rows.append(of[pl.ds(block * 4 * Z + (k // HZ) * 2 * Z + k % HZ, 4, stride=HZ), :])
        rows = jnp.concatenate(rows, axis=0).astype(BF)
        out_ref[:, pl.ds(mod(z + order[k], Z), 1), :] = jnp.dot(
            osel[...], rows, preferred_element_type=F32
        )[:, None, :]


def body(spectra, home, lists, Y, Z):
    dft, sel_s, sel_r, block, band = (jnp.asarray(t) for t in tables())
    vmem = pl.BlockSpec(memory_space=pltpu.VMEM)
    dma = pltpu.SemaphoreType.DMA
    HY = Y // 2
    out = pl.pallas_call(
        functools.partial(kernel, Y, Z),
        out_shape=jax.ShapeDtypeStruct((LIST, Z, LAGS), F32),
        in_specs=[pl.BlockSpec(memory_space=pl.ANY)] * 8,
        out_specs=vmem,
        scratch_shapes=[
            pltpu.VMEM((W, 4, 2 * F), BF),
            pltpu.VMEM((2, 128), jnp.int32),
            pltpu.VMEM((1, LIST), jnp.int32),
            pltpu.VMEM(dft.shape, BF),
            pltpu.VMEM(sel_s.shape, BF),
            pltpu.VMEM(sel_r.shape, F32),
            pltpu.VMEM(block.shape, F32),
            pltpu.VMEM(band.shape, BF),
            pltpu.VMEM((48, 1024), F32),
            pltpu.VMEM((2, 48, 128), F32),
            pltpu.VMEM((2, Y, 2, 48, 512), BF),
            pltpu.VMEM((Z, X, 2, 48, 128), BF),
            pltpu.VMEM((X, 8, 128), F32),
            pltpu.VMEM((Z, W, 16, F), BF),
            pltpu.VMEM((Z, W, 16, F), BF),
            pltpu.VMEM((2 * Y, W, 2, 16, F), BF),
            pltpu.VMEM((2 * Z, 8, 128), F32),
            pltpu.VMEM((X, 2, 16 * Z, 128), BF),
            pltpu.VMEM((X, 2, 16 * Z, 128), BF),
            pltpu.VMEM((128 * Z, 128), F32),
            pltpu.VMEM((128, 128), BF),
            dma((8,)),
            dma((2, HY, 2)), dma((2, HY, 2)),
            dma((Y, 2)), dma((Y, 2)),
            dma((X - 1,)), dma((X - 1,)),
            dma((2,)), dma((2,)),
            dma((Z - 1,)), dma((Z - 1,)),
            dma((X - 1, Z)), dma((X - 1, Z)),
            dma((X - 1, Y)), dma((X - 1, Y)),
        ],
        compiler_params=pltpu.CompilerParams(
            collective_id=0, has_side_effects=True, vmem_limit_bytes=60 * 2**20
        ),
        cost_estimate=pl.CostEstimate(
            flops=6_500_000_000, bytes_accessed=4_000_000, transcendentals=400_000
        ),
    )(spectra.transpose(1, 2, 0, 3)[0], home.reshape(2, 128), lists, dft, sel_s, sel_r, block, band)
    return out[None, :, :, None, :]


def solution(mesh):
    Y = mesh.shape["src"] // (2 * X)
    Z = mesh.shape["rcv"]
    return jax.shard_map(
        functools.partial(body, Y=Y, Z=Z),
        mesh=mesh,
        in_specs=(P("src", "rcv", None, None), P(), P("src", None)),
        out_specs=P("src", None, None, "rcv", None),
        check_vma=False,
    )
```

```python
import functools
import math

import jax
import jax.numpy as jnp
import numpy as np
from jax import lax
from jax.experimental import pallas as pl
from jax.experimental.pallas import tpu as pltpu
from jax.sharding import PartitionSpec as P

F = 2048
LAGS = 128
W = 3
BAND = 32
LIST = 128
X = 4
FT = 2048
BF = jnp.bfloat16
F32 = jnp.float32
MESH = pl.DeviceIdType.MESH


def tables():
    freq = np.arange(F, dtype=np.int64)[:, None]
    lag = np.arange(LAGS, dtype=np.int64)[None, :] - LAGS // 2
    angle = ((freq * lag) % (2 * F)).astype(np.float64) * (math.pi / F)
    dft = np.concatenate([np.cos(angle), np.sin(angle)], axis=1) / math.sqrt(F)
    sel_s = np.zeros((16, W, 8, X, 16, W), np.float32)
    for r in range(8):
        for q in range(16):
            for w in range(W):
                sel_s[q, w, r, r // 2, q, w] = 1
    sel_r = np.zeros((4, W, 8, 4, W, 4), np.float32)
    for q in range(4):
        for w in range(W):
            sel_r[q, w, :, q, w, :] = 1
    block = np.zeros((8, 4, W, 4), np.float32) + np.arange(4)[None, None, None, :]
    lanes = np.arange(128)
    band = (lanes[:, None] // BAND == lanes[None, :] // BAND) / BAND
    return (
        dft.astype(np.float32).astype(BF),
        sel_s.reshape(16 * W * 8, X * 16 * W).astype(BF),
        sel_r.reshape(4 * W * 8, 4 * 4 * W),
        block.reshape(8, 4 * 4 * W),
        band.astype(BF),
    )


def exact_dot(a, b):
    hi = a.astype(BF)
    rest = a - hi.astype(F32)
    mid = rest.astype(BF)
    low = (rest - mid.astype(F32)).astype(BF)
    dot = functools.partial(jnp.dot, preferred_element_type=F32)
    return dot(hi, b) + dot(mid, b) + dot(low, b)


def kernel(
    Y, Z,
    spec_hbm, home_hbm, lists_hbm, dft_hbm, sel_s_hbm, sel_r_hbm, block_hbm, band_hbm,
    out_ref,
    spec_ref, home_ref, lists_ref, dft, sel_s_ref, sel_r_ref, block_ref, band_ref,
    rf, sf, rbuf, sbuf, gbuf, ubuf, vbuf, rg, tbuf, rbuf32, obuf, ibuf, of, osel,
    in_sem, yss, yrs, qss, qrs, gss, grs, nss, nrs, zss, zrs, xss, xrs, oss, ors,
):
    HY, HZ = Y // 2, Z // 2
    src = lax.axis_index("src")
    z = lax.axis_index("rcv")
    c = lax.rem(src, 2)
    y = lax.rem(src // 2, Y)
    x = src // (2 * Y)
    order = [0]
    for d in range(1, HZ + 1):
        order += sorted({d, Z - d})

    def dev(xx, yy, cc, zz):
        return ((xx * Y + yy) * 2 + cc, zz)

    def mod(a, n):
        return lax.rem(a + n, n)

    def remote(a, b, ss, rs, device):
        return pltpu.make_async_remote_copy(
            src_ref=a, dst_ref=b, send_sem=ss, recv_sem=rs, device_id=device, device_id_type=MESH
        )

    barrier = pltpu.get_barrier_semaphore()
    peers = [dev(x, y, 1 - c, z)]
    peers += [dev(x, mod(y + 1, Y), c, z), dev(x, mod(y - 1, Y), c, z)]
    peers += [dev(mod(x + d, X), y, c, z) for d in range(1, X)]
    peers += [dev(x, y, c, mod(z + d, Z)) for d in range(1, Z)]
    for peer in peers:
        pl.semaphore_signal(barrier, inc=1, device_id=peer, device_id_type=MESH)

    loads = [
        pltpu.make_async_copy(a, b, in_sem.at[k])
        for k, (a, b) in enumerate((
            (spec_hbm, spec_ref), (band_hbm, band_ref), (home_hbm, home_ref),
            (lists_hbm, lists_ref), (sel_s_hbm, sel_s_ref), (sel_r_hbm, sel_r_ref),
            (block_hbm, block_ref), (dft_hbm, dft),
        ))
    ]
    for load in loads:
        load.start()
    if Y < 8:
        ibuf[...] = jnp.zeros_like(ibuf)
        obuf[...] = jnp.zeros_like(obuf)
    loads[0].wait()
    loads[1].wait()

    pad = jnp.zeros((4, F), F32)
    spectra, energies = [], []
    for w in range(W):
        s = spec_ref[w].astype(F32)
        spectra.append(s)
        e = s[:, :F] * s[:, :F] + s[:, F:] * s[:, F:]
        e = jnp.concatenate([e, pad], axis=0)
        energies += [e[:, t * 128 : t * 128 + 128] for t in range(16)]
    mean = exact_dot(jnp.concatenate(energies, axis=0), band_ref[...])
    scale = lax.rsqrt(mean + 1e-05)
    for w in range(W):
        for t in range(16):
            k = scale[(w * 16 + t) * 8 : (w * 16 + t) * 8 + 4]
            for part in range(2):
                v = spectra[w][:, part * F + t * 128 : part * F + t * 128 + 128] * k
                q, lane = part * 2 + t // 8, (t % 8) * 128
                rf[pl.ds(q * 12 + w * 4, 4), pl.ds(lane, 128)] = v
                sf[part, pl.ds(t * 3 + w, 1), :] = v[:1]
    whitened = rf[...].astype(BF)
    for h in range(2):
        rbuf[c, y, h] = whitened[:, h * 512 : h * 512 + 512]
    sbuf[z, x] = sf[...].astype(BF)

    pl.semaphore_wait(barrier, len(peers))

    started = []

    def start(copy):
        copy.start()
        started.append(copy)

    def x_peer(d):
        return dev(mod(x + d, X), y, c, z)

    def y_copy(way, d, h, arrival=False):
        e = d + 1 if arrival else d
        at = mod(y - e, Y) if way == 0 else mod(y + e, Y)
        to = mod(y + 1, Y) if way == 0 else mod(y - 1, Y)
        ref = rbuf.at[c, at, h]
        return remote(ref, ref, yss.at[way, d, h], yrs.at[way, d, h], dev(x, to, c, z))

    def y_pieces(way, d):
        return (0, 1) if d + 1 < HY else ((way,) if d + 1 == HY else ())

    def q_copy(rel, h, core):
        ref = rbuf.at[core, mod(y + rel, Y), h]
        return remote(ref, ref, qss.at[rel, h], qrs.at[rel, h], dev(x, y, 1 - c, z))

    def g_copy(d, origin):
        ref = gbuf.at[origin]
        return remote(ref, ref, gss.at[d - 1], grs.at[d - 1], x_peer(d))

    def z_copy(d, origin):
        ref = sbuf.at[origin, x]
        return remote(ref, ref, zss.at[d - 1], zrs.at[d - 1], dev(x, y, c, mod(z + d, Z)))

    def near_copy(way, origin):
        to = mod(z + 1, Z) if way == 0 else mod(z - 1, Z)
        ref = sbuf.at[origin]
        return remote(ref, ref, nss.at[way], nrs.at[way], dev(x, y, c, to))

    def x_copy(d, rel, origin):
        ref = sbuf.at[mod(z + rel, Z), origin]
        return remote(ref, ref, xss.at[d - 1, rel], xrs.at[d - 1, rel], x_peer(d))

    GZ = Z // 4
    M = 4 * GZ

    def o_copy(d, m, arrival=False):
        rows = pl.ds(pl.multiple_of(m * 4 * Z, 4 * Z), 4 * Z)
        a = ibuf.at[mod(x - d, X), :, rows] if arrival else obuf.at[mod(x + d, X), :, rows]
        b = ibuf.at[mod(x - d, X) if arrival else x, :, rows]
        return remote(a, b, oss.at[d - 1, m], ors.at[d - 1, m], x_peer(d))

    near = (1, Z - 1) if Z > 2 else ()
    far = [d for d in order[1:] if d not in near]
    for d in far:
        start(z_copy(d, z))
    for d in range(1, X):
        start(x_copy(d, 0, x))
    for way in range(2):
        for h in y_pieces(way, 0):
            start(y_copy(way, 0, h))
    for h in range(2):
        start(q_copy(0, h, c))

    for load in loads[2:]:
        load.wait()
    sub = lax.broadcasted_iota(jnp.int32, (128, 128), 0)
    listed = lists_ref[...]
    home = home_ref[...].astype(F32)
    pos = jnp.zeros((1, 128), F32)
    for h in range(2):
        column = jnp.transpose(jnp.broadcast_to(home[h : h + 1], (128, 128)))
        hit = listed == sub + h * 128
        pos = pos + jnp.sum(jnp.where(hit, column, 0.0), axis=0, keepdims=True)
    pos = jnp.where(listed >= 0, pos, -1.0)
    pos = jnp.transpose(jnp.broadcast_to(pos, (128, 128)))
    lane = lax.broadcasted_iota(jnp.int32, (1, 128), 1)
    lane_c = (lane >> 4) & 1
    lane_n = (lane >> 1) & 7
    lane_y = (y + jnp.where((lane_n & 1) == 1, (lane_n + 1) >> 1, Y - (lane_n >> 1))) & (Y - 1)
    base = ((((lane >> 5) * Y + lane_y) * 2 + (lane & 1)) * 4).astype(F32)
    base = jnp.where(lane_n < Y, base, -100.0)
    has = [
        jnp.max(jnp.where(pos == base + b, 1.0, 0.0), axis=0, keepdims=True) > 0.5
        for b in range(4)
    ]
    first = jnp.where(has[0], 0.0, jnp.where(has[1], 1.0, jnp.where(has[2], 2.0, 3.0)))
    last = jnp.where(has[3], 3.0, jnp.where(has[2], 2.0, jnp.where(has[1], 1.0, 0.0)))
    pick = jnp.where(lane_c == 1, last, first)
    target = jnp.where((lane_c == 1) & (first == last), -50.0, base + pick)
    osel[...] = jnp.where(pos == target, 1.0, 0.0).astype(BF)
    gbuf[x] = jnp.broadcast_to(pick, (8, 128))

    for d in range(1, X):
        start(g_copy(d, x))

    def z_step(rel):
        z_copy(Z - rel, mod(z + rel, Z)).wait_recv()
        for k in range(1, X):
            start(x_copy(k, rel, x))

    def y_step(d, send):
        for way in range(2):
            for h in y_pieces(way, d - 1):
                y_copy(way, d - 1, h, arrival=True).wait_recv()
                if h in y_pieces(way, d):
                    send(y_copy(way, d, h))
                send(q_copy(Y - d if way == 0 else d, h, c))

    def assemble(k):
        rel = order[k]
        at = mod(z + rel, Z)
        if rel in near:
            near_copy(near.index(rel) ^ 1, at).wait_recv()
        elif rel:
            for d in range(1, X):
                x_copy(d, rel, mod(x - d, X)).wait_recv()
        parts = sbuf[at]
        parts = jnp.concatenate(
            [parts[:, 0].reshape(X * 48, 128), parts[:, 1].reshape(X * 48, 128)], axis=1
        )
        rows = jnp.dot(sel_s_ref[...], parts, preferred_element_type=F32)
        for q in range(16):
            for w in range(W):
                v = rows[(q * W + w) * 8 : (q * W + w) * 8 + 8]
                re, im = v[:, :128], v[:, 128:]
                ubuf[k, w, :, pl.ds(q * 128, 128)] = jnp.concatenate([re, im], axis=0).astype(BF)
                vbuf[k, w, :, pl.ds(q * 128, 128)] = jnp.concatenate([im, -re], axis=0).astype(BF)

    NM = HY
    steps = [(0, 0), (0, 1), (1, 0), (1, 1), (2, 0), (2, 1), (0, 2), (1, 2), (2, 2)]
    steps += [(3, 0), (3, 1), (3, 2)] + [(g, 3) for g in range(4)]
    for d in range(1, X):
        x_copy(d, 0, mod(x - d, X)).wait_recv()
    for way in range(2):
        start(near_copy(way, z))
    y_step(1, start)
    assemble(0)
    for rel in far:
        z_step(rel)
    y_step(2, start)
    for k in range(1, GZ):
        assemble(k)
    for d in range(1, X):
        g_copy(d, mod(x - d, X)).wait_recv()

    g_rows = lax.broadcasted_iota(jnp.int32, (8, 128), 0)
    g_lanes = lax.broadcasted_iota(jnp.int32, (8, 128), 1)
    picks = gbuf[0]
    for s in range(1, X):
        picks = jnp.where((g_rows >> 1) == s, gbuf[s], picks)

    def begin(copy):
        copy.start()

    @pl.loop(0, len(steps))
    def _(t):
        group = m = 0
        for k, (g, at) in enumerate(steps):
            group = jnp.where(t == k, g, group)
            m = jnp.where(t == k, at, m)
        for d, when in ((3, 3), (4, 8)):

            @pl.when(t == when)
            def _(d=d):
                y_step(d, begin)

        for g in range(1, 4):

            @pl.when(t == steps.index((g, 0)))
            def _(g=g):
                for k in range(g * GZ, g * GZ + GZ):
                    assemble(k)

        @pl.when(group == 0)
        def _():
            for u in range(2):
                n = 2 * m + u
                rel = jnp.where(u == 1, m + 1, lax.rem(Y - m, Y))
                at = mod(y + rel, Y)
                for h in range(2):
                    q_copy(rel, h, 1 - c).wait_recv()
                for core in range(2):
                    mark = x * 32 + (g_rows & 1) * 16 + n * 2 + core
                    column = jnp.sum(jnp.where(g_lanes == mark, picks, 0.0), axis=1, keepdims=True)
                    sel = jnp.where(block_ref[...] == column, 1.0, 0.0)
                    sel = (jnp.concatenate([sel] * 12, axis=0) * sel_r_ref[...]).astype(BF)
                    for h in range(2):
                        rows = jnp.dot(sel, rbuf[core, at, h], preferred_element_type=F32)
                        for q in range(4):
                            for w in range(W):
                                v = rows[(q * W + w) * 8 : (q * W + w) * 8 + 8]
                                rg[2 * n + core, w, q // 2, :, pl.ds((q % 2) * 1024 + h * 512, 512)] = (
                                    jnp.concatenate([v, v], axis=0).astype(BF)
                                )

        signal = None
        for f in range(0, F, FT):
            fs = pl.ds(f, FT)
            rows = []
            for w in range(W):
                for u in range(4):
                    rr, ri = rg[4 * m + u, w, 0, :, fs], rg[4 * m + u, w, 1, :, fs]
                    for k in range(GZ):
                        i = group * GZ + k
                        rows.append(ubuf[i, w, :, fs] * rr + vbuf[i, w, :, fs] * ri)
            part = jnp.dot(jnp.concatenate(rows, axis=0), dft[fs, :], preferred_element_type=F32)
            signal = part if signal is None else signal + part
        signal = signal.reshape(W, M, 2, 8, 256)
        real = signal[:, :, 0, :, :128] - signal[:, :, 1, :, 128:]
        imag = signal[:, :, 0, :, 128:] + signal[:, :, 1, :, :128]
        energy = real * real + imag * imag
        inverse = lax.rsqrt(energy + (0.1 * jnp.mean(energy, axis=-1, keepdims=True) + 1e-05))
        pr, pi = real * inverse, imag * inverse
        third = 1.0 / 3.0
        mr = (pr[0] + pr[1] + pr[2]) * third
        mi = (pi[0] + pi[1] + pi[2]) * third
        tbuf[...] = ((real[0] + real[1] + real[2]) * third) * (mr * mr + mi * mi)
        at_rows = pl.ds(pl.multiple_of(m * 4 * Z + group * M, M), M)
        for s in range(X):
            for k in range(2):
                rbuf32[s, k, at_rows, :] = tbuf[:, 2 * s + k, :]

        @pl.when(group == 3)
        def _():
            all_rows = pl.ds(pl.multiple_of(m * 4 * Z, 4 * Z), 4 * Z)
            for s in range(X):
                for k in range(2):
                    obuf[s, k, all_rows, :] = rbuf32[s, k, all_rows, :].astype(BF)
            for d in range(1, X):
                o_copy(d, m).start()

    for copy in started:
        copy.wait_send()
    for d in sorted({HY, 3} if HY > 3 else {HY}):
        for way in range(2):
            for h in y_pieces(way, d - 1):
                if h in y_pieces(way, d):
                    y_copy(way, d, h).wait_send()
                q_copy(Y - d if way == 0 else d, h, c).wait_send()
    ibuf[x] = obuf[x]
    for d in range(1, X):
        for m in range(NM):
            o_copy(d, m).wait_send()
            o_copy(d, m, arrival=True).wait_recv()
    of[...] = ibuf[...].astype(F32).reshape(X * 2 * 8 * 2 * Z, 128)
    for k in range(Z):
        rows = []
        for block in range(X * 2 * 4):
            rows.append(of[pl.ds(block * 4 * Z + (k // GZ) * M + k % GZ, 4, stride=GZ), :])
        rows = jnp.concatenate(rows, axis=0).astype(BF)
        out_ref[:, pl.ds(mod(z + order[k], Z), 1), :] = jnp.dot(
            osel[...], rows, preferred_element_type=F32
        )[:, None, :]


def body(spectra, home, lists, Y, Z):
    dft, sel_s, sel_r, block, band = (jnp.asarray(t) for t in tables())
    vmem = pl.BlockSpec(memory_space=pltpu.VMEM)
    dma = pltpu.SemaphoreType.DMA
    HY = Y // 2
    out = pl.pallas_call(
        functools.partial(kernel, Y, Z),
        out_shape=jax.ShapeDtypeStruct((LIST, Z, LAGS), F32),
        in_specs=[pl.BlockSpec(memory_space=pl.ANY)] * 8,
        out_specs=vmem,
        scratch_shapes=[
            pltpu.VMEM((W, 4, 2 * F), BF),
            pltpu.VMEM((2, 128), jnp.int32),
            pltpu.VMEM((1, LIST), jnp.int32),
            pltpu.VMEM(dft.shape, BF),
            pltpu.VMEM(sel_s.shape, BF),
            pltpu.VMEM(sel_r.shape, F32),
            pltpu.VMEM(block.shape, F32),
            pltpu.VMEM(band.shape, BF),
            pltpu.VMEM((48, 1024), F32),
            pltpu.VMEM((2, 48, 128), F32),
            pltpu.VMEM((2, Y, 2, 48, 512), BF),
            pltpu.VMEM((Z, X, 2, 48, 128), BF),
            pltpu.VMEM((X, 8, 128), F32),
            pltpu.VMEM((Z, W, 16, F), BF),
            pltpu.VMEM((Z, W, 16, F), BF),
            pltpu.VMEM((2 * Y, W, 2, 16, F), BF),
            pltpu.VMEM((Z, 8, 128), F32),
            pltpu.VMEM((X, 2, 16 * Z, 128), F32),
            pltpu.VMEM((X, 2, 16 * Z, 128), BF),
            pltpu.VMEM((X, 2, 16 * Z, 128), BF),
            pltpu.VMEM((128 * Z, 128), F32),
            pltpu.VMEM((128, 128), BF),
            dma((8,)),
            dma((2, HY, 2)), dma((2, HY, 2)),
            dma((Y, 2)), dma((Y, 2)),
            dma((X - 1,)), dma((X - 1,)),
            dma((2,)), dma((2,)),
            dma((Z - 1,)), dma((Z - 1,)),
            dma((X - 1, Z)), dma((X - 1, Z)),
            dma((X - 1, Y // 2)), dma((X - 1, Y // 2)),
        ],
        compiler_params=pltpu.CompilerParams(
            collective_id=0, has_side_effects=True, vmem_limit_bytes=60 * 2**20
        ),
        cost_estimate=pl.CostEstimate(
            flops=6_500_000_000, bytes_accessed=4_000_000, transcendentals=400_000
        ),
    )(spectra.transpose(1, 2, 0, 3)[0], home.reshape(2, 128), lists, dft, sel_s, sel_r, block, band)
    return out[None, :, :, None, :]


def solution(mesh):
    Y = mesh.shape["src"] // (2 * X)
    Z = mesh.shape["rcv"]
    return jax.shard_map(
        functools.partial(body, Y=Y, Z=Z),
        mesh=mesh,
        in_specs=(P("src", "rcv", None, None), P(), P("src", None)),
        out_specs=P("src", None, None, "rcv", None),
        check_vma=False,
    )
```

```python
import functools
import math

import jax
import jax.numpy as jnp
import numpy as np
from jax import lax
from jax.experimental import pallas as pl
from jax.experimental.pallas import tpu as pltpu
from jax.sharding import PartitionSpec as P

F = 2048
LAGS = 128
W = 3
BAND = 32
LIST = 128
X = 4
FT = 2048
BF = jnp.bfloat16
F32 = jnp.float32
MESH = pl.DeviceIdType.MESH


def tables():
    freq = np.arange(F, dtype=np.int64)[:, None]
    lag = np.arange(LAGS, dtype=np.int64)[None, :] - LAGS // 2
    angle = ((freq * lag) % (2 * F)).astype(np.float64) * (math.pi / F)
    dft = np.concatenate([np.cos(angle), np.sin(angle)], axis=1) / math.sqrt(F)
    sel_s = np.zeros((16, W, 8, X, 16, W), np.float32)
    for r in range(8):
        for q in range(16):
            for w in range(W):
                sel_s[q, w, r, r // 2, q, w] = 1
    sel_r = np.zeros((4, W, 8, 4, W, 4), np.float32)
    for q in range(4):
        for w in range(W):
            sel_r[q, w, :, q, w, :] = 1
    block = np.zeros((8, 4, W, 4), np.float32) + np.arange(4)[None, None, None, :]
    lanes = np.arange(128)
    band = (lanes[:, None] // BAND == lanes[None, :] // BAND) / BAND
    return (
        dft.astype(np.float32).astype(BF),
        sel_s.reshape(16 * W * 8, X * 16 * W).astype(BF),
        sel_r.reshape(4 * W * 8, 4 * 4 * W),
        block.reshape(8, 4 * 4 * W),
        band.astype(BF),
    )


def exact_dot(a, b):
    hi = a.astype(BF)
    rest = a - hi.astype(F32)
    mid = rest.astype(BF)
    low = (rest - mid.astype(F32)).astype(BF)
    dot = functools.partial(jnp.dot, preferred_element_type=F32)
    return dot(hi, b) + dot(mid, b) + dot(low, b)


def kernel(
    Y, Z,
    spec_hbm, home_hbm, lists_hbm, dft_hbm, sel_s_hbm, sel_r_hbm, block_hbm, band_hbm,
    out_ref,
    spec_ref, home_ref, lists_ref, dft, sel_s_ref, sel_r_ref, block_ref, band_ref,
    rf, sf, rbuf, sbuf, gbuf, ubuf, vbuf, rg, tbuf, rbuf32, obuf, ibuf, of, osel,
    in_sem, yss, yrs, qss, qrs, gss, grs, nss, nrs, zss, zrs, xss, xrs, oss, ors,
):
    HY, HZ = Y // 2, Z // 2
    src = lax.axis_index("src")
    z = lax.axis_index("rcv")
    c = lax.rem(src, 2)
    y = lax.rem(src // 2, Y)
    x = src // (2 * Y)
    order = [0]
    for d in range(1, HZ + 1):
        order += sorted({d, Z - d})

    def dev(xx, yy, cc, zz):
        return ((xx * Y + yy) * 2 + cc, zz)

    def mod(a, n):
        return lax.rem(a + n, n)

    def remote(a, b, ss, rs, device):
        return pltpu.make_async_remote_copy(
            src_ref=a, dst_ref=b, send_sem=ss, recv_sem=rs, device_id=device, device_id_type=MESH
        )

    barrier = pltpu.get_barrier_semaphore()
    peers = [dev(x, y, 1 - c, z)]
    peers += [dev(x, mod(y + 1, Y), c, z), dev(x, mod(y - 1, Y), c, z)]
    peers += [dev(mod(x + d, X), y, c, z) for d in range(1, X)]
    peers += [dev(x, y, c, mod(z + d, Z)) for d in range(1, Z)]
    for peer in peers:
        pl.semaphore_signal(barrier, inc=1, device_id=peer, device_id_type=MESH)

    loads = [
        pltpu.make_async_copy(a, b, in_sem.at[k])
        for k, (a, b) in enumerate((
            (spec_hbm, spec_ref), (band_hbm, band_ref), (home_hbm, home_ref),
            (lists_hbm, lists_ref), (sel_s_hbm, sel_s_ref), (sel_r_hbm, sel_r_ref),
            (block_hbm, block_ref), (dft_hbm, dft),
        ))
    ]
    for load in loads:
        load.start()
    if Y < 8:
        ibuf[...] = jnp.zeros_like(ibuf)
        obuf[...] = jnp.zeros_like(obuf)
    loads[0].wait()
    loads[1].wait()

    pad = jnp.zeros((4, F), F32)
    spectra, energies = [], []
    for w in range(W):
        s = spec_ref[w].astype(F32)
        spectra.append(s)
        e = s[:, :F] * s[:, :F] + s[:, F:] * s[:, F:]
        e = jnp.concatenate([e, pad], axis=0)
        energies += [e[:, t * 128 : t * 128 + 128] for t in range(16)]
    mean = exact_dot(jnp.concatenate(energies, axis=0), band_ref[...])
    scale = lax.rsqrt(mean + 1e-05)
    for w in range(W):
        for t in range(16):
            k = scale[(w * 16 + t) * 8 : (w * 16 + t) * 8 + 4]
            for part in range(2):
                v = spectra[w][:, part * F + t * 128 : part * F + t * 128 + 128] * k
                q, lane = part * 2 + t // 8, (t % 8) * 128
                rf[pl.ds(q * 12 + w * 4, 4), pl.ds(lane, 128)] = v
                sf[part, pl.ds(t * 3 + w, 1), :] = v[:1]
    whitened = rf[...].astype(BF)
    for h in range(2):
        rbuf[c, y, h] = whitened[:, h * 512 : h * 512 + 512]
    sbuf[z, x] = sf[...].astype(BF)

    pl.semaphore_wait(barrier, len(peers))

    started = []

    def start(copy):
        copy.start()
        started.append(copy)

    def x_peer(d):
        return dev(mod(x + d, X), y, c, z)

    def y_copy(way, d, h, arrival=False):
        e = d + 1 if arrival else d
        at = mod(y - e, Y) if way == 0 else mod(y + e, Y)
        to = mod(y + 1, Y) if way == 0 else mod(y - 1, Y)
        ref = rbuf.at[c, at, h]
        return remote(ref, ref, yss.at[way, d, h], yrs.at[way, d, h], dev(x, to, c, z))

    def y_pieces(way, d):
        return (0, 1) if d + 1 < HY else ((way,) if d + 1 == HY else ())

    def q_copy(rel, h, core):
        ref = rbuf.at[core, mod(y + rel, Y), h]
        return remote(ref, ref, qss.at[rel, h], qrs.at[rel, h], dev(x, y, 1 - c, z))

    def g_copy(d, origin):
        ref = gbuf.at[origin]
        return remote(ref, ref, gss.at[d - 1], grs.at[d - 1], x_peer(d))

    def z_copy(d, origin):
        ref = sbuf.at[origin, x]
        return remote(ref, ref, zss.at[d - 1], zrs.at[d - 1], dev(x, y, c, mod(z + d, Z)))

    def near_copy(way, origin):
        to = mod(z + 1, Z) if way == 0 else mod(z - 1, Z)
        ref = sbuf.at[origin]
        return remote(ref, ref, nss.at[way], nrs.at[way], dev(x, y, c, to))

    def x_copy(d, rel, origin):
        ref = sbuf.at[mod(z + rel, Z), origin]
        return remote(ref, ref, xss.at[d - 1, rel], xrs.at[d - 1, rel], x_peer(d))

    GZ = Z // 4
    M = 4 * GZ

    def o_copy(d, m, arrival=False):
        rows = pl.ds(pl.multiple_of(m * 4 * Z, 4 * Z), 4 * Z)
        a = ibuf.at[mod(x - d, X), :, rows] if arrival else obuf.at[mod(x + d, X), :, rows]
        b = ibuf.at[mod(x - d, X) if arrival else x, :, rows]
        return remote(a, b, oss.at[d - 1, m], ors.at[d - 1, m], x_peer(d))

    near = (1, Z - 1) if Z > 2 else ()
    far = [d for d in order[1:] if d not in near]
    for d in far:
        start(z_copy(d, z))
    for d in range(1, X):
        start(x_copy(d, 0, x))
    for way in range(2):
        for h in y_pieces(way, 0):
            start(y_copy(way, 0, h))
    for h in range(2):
        start(q_copy(0, h, c))

    for load in loads[2:]:
        load.wait()
    sub = lax.broadcasted_iota(jnp.int32, (128, 128), 0)
    listed = lists_ref[...]
    home = home_ref[...].astype(F32)
    pos = jnp.zeros((1, 128), F32)
    for h in range(2):
        column = jnp.transpose(jnp.broadcast_to(home[h : h + 1], (128, 128)))
        hit = listed == sub + h * 128
        pos = pos + jnp.sum(jnp.where(hit, column, 0.0), axis=0, keepdims=True)
    pos = jnp.where(listed >= 0, pos, -1.0)
    pos = jnp.transpose(jnp.broadcast_to(pos, (128, 128)))
    lane = lax.broadcasted_iota(jnp.int32, (1, 128), 1)
    lane_c = (lane >> 4) & 1
    lane_n = (lane >> 1) & 7
    lane_y = (y + jnp.where((lane_n & 1) == 1, (lane_n + 1) >> 1, Y - (lane_n >> 1))) & (Y - 1)
    base = ((((lane >> 5) * Y + lane_y) * 2 + (lane & 1)) * 4).astype(F32)
    base = jnp.where(lane_n < Y, base, -100.0)
    has = [
        jnp.max(jnp.where(pos == base + b, 1.0, 0.0), axis=0, keepdims=True) > 0.5
        for b in range(4)
    ]
    first = jnp.where(has[0], 0.0, jnp.where(has[1], 1.0, jnp.where(has[2], 2.0, 3.0)))
    last = jnp.where(has[3], 3.0, jnp.where(has[2], 2.0, jnp.where(has[1], 1.0, 0.0)))
    pick = jnp.where(lane_c == 1, last, first)
    target = jnp.where((lane_c == 1) & (first == last), -50.0, base + pick)
    osel[...] = jnp.where(pos == target, 1.0, 0.0).astype(BF)
    gbuf[x] = jnp.broadcast_to(pick, (8, 128))

    for d in range(1, X):
        start(g_copy(d, x))

    def z_step(rel):
        z_copy(Z - rel, mod(z + rel, Z)).wait_recv()
        for k in range(1, X):
            start(x_copy(k, rel, x))

    def y_step(d, send):
        for way in range(2):
            for h in y_pieces(way, d - 1):
                y_copy(way, d - 1, h, arrival=True).wait_recv()
                if h in y_pieces(way, d):
                    send(y_copy(way, d, h))
                send(q_copy(Y - d if way == 0 else d, h, c))

    def assemble(k):
        rel = order[k]
        at = mod(z + rel, Z)
        if rel in near:
            near_copy(near.index(rel) ^ 1, at).wait_recv()
        elif rel:
            for d in range(1, X):
                x_copy(d, rel, mod(x - d, X)).wait_recv()
        parts = sbuf[at]
        parts = jnp.concatenate(
            [parts[:, 0].reshape(X * 48, 128), parts[:, 1].reshape(X * 48, 128)], axis=1
        )
        rows = jnp.dot(sel_s_ref[...], parts, preferred_element_type=F32)
        for q in range(16):
            for w in range(W):
                v = rows[(q * W + w) * 8 : (q * W + w) * 8 + 8]
                re, im = v[:, :128], v[:, 128:]
                ubuf[k, w, :, pl.ds(q * 128, 128)] = jnp.concatenate([re, im], axis=0).astype(BF)
                vbuf[k, w, :, pl.ds(q * 128, 128)] = jnp.concatenate([im, -re], axis=0).astype(BF)

    NM = HY
    steps = [(0, 0), (0, 1), (1, 0), (1, 1), (2, 0), (2, 1), (3, 0), (3, 1)]
    steps += [(g, 2) for g in range(4)] + [(g, 3) for g in range(4)]
    for d in range(1, X):
        x_copy(d, 0, mod(x - d, X)).wait_recv()
    for way in range(2):
        start(near_copy(way, z))
    y_step(1, start)
    assemble(0)
    for rel in far:
        z_step(rel)
    y_step(2, start)
    for k in range(1, GZ):
        assemble(k)
    for d in range(1, X):
        g_copy(d, mod(x - d, X)).wait_recv()

    g_rows = lax.broadcasted_iota(jnp.int32, (8, 128), 0)
    g_lanes = lax.broadcasted_iota(jnp.int32, (8, 128), 1)
    picks = gbuf[0]
    for s in range(1, X):
        picks = jnp.where((g_rows >> 1) == s, gbuf[s], picks)

    def begin(copy):
        copy.start()

    @pl.loop(0, len(steps))
    def _(t):
        group = m = 0
        for k, (g, at) in enumerate(steps):
            group = jnp.where(t == k, g, group)
            m = jnp.where(t == k, at, m)
        for d, when in ((3, 4), (4, 9)):

            @pl.when(t == when)
            def _(d=d):
                y_step(d, begin)

        for g in range(1, 4):

            @pl.when(t == steps.index((g, 0)))
            def _(g=g):
                for k in range(g * GZ, g * GZ + GZ):
                    assemble(k)

        @pl.when(group == 0)
        def _():
            for u in range(2):
                n = 2 * m + u
                rel = jnp.where(u == 1, m + 1, lax.rem(Y - m, Y))
                at = mod(y + rel, Y)
                for h in range(2):
                    q_copy(rel, h, 1 - c).wait_recv()
                for core in range(2):
                    mark = x * 32 + (g_rows & 1) * 16 + n * 2 + core
                    column = jnp.sum(jnp.where(g_lanes == mark, picks, 0.0), axis=1, keepdims=True)
                    sel = jnp.where(block_ref[...] == column, 1.0, 0.0)
                    sel = (jnp.concatenate([sel] * 12, axis=0) * sel_r_ref[...]).astype(BF)
                    for h in range(2):
                        rows = jnp.dot(sel, rbuf[core, at, h], preferred_element_type=F32)
                        for q in range(4):
                            for w in range(W):
                                v = rows[(q * W + w) * 8 : (q * W + w) * 8 + 8]
                                rg[2 * n + core, w, q // 2, :, pl.ds((q % 2) * 1024 + h * 512, 512)] = (
                                    jnp.concatenate([v, v], axis=0).astype(BF)
                                )

        signal = None
        for f in range(0, F, FT):
            fs = pl.ds(f, FT)
            rows = []
            for w in range(W):
                for u in range(4):
                    rr, ri = rg[4 * m + u, w, 0, :, fs], rg[4 * m + u, w, 1, :, fs]
                    for k in range(GZ):
                        i = group * GZ + k
                        rows.append(ubuf[i, w, :, fs] * rr + vbuf[i, w, :, fs] * ri)
            part = jnp.dot(jnp.concatenate(rows, axis=0), dft[fs, :], preferred_element_type=F32)
            signal = part if signal is None else signal + part
        signal = signal.reshape(W, M, 2, 8, 256)
        real = signal[:, :, 0, :, :128] - signal[:, :, 1, :, 128:]
        imag = signal[:, :, 0, :, 128:] + signal[:, :, 1, :, :128]
        energy = real * real + imag * imag
        inverse = lax.rsqrt(energy + (0.1 * jnp.mean(energy, axis=-1, keepdims=True) + 1e-05))
        pr, pi = real * inverse, imag * inverse
        third = 1.0 / 3.0
        mr = (pr[0] + pr[1] + pr[2]) * third
        mi = (pi[0] + pi[1] + pi[2]) * third
        tbuf[...] = ((real[0] + real[1] + real[2]) * third) * (mr * mr + mi * mi)
        at_rows = pl.ds(pl.multiple_of(m * 4 * Z + group * M, M), M)
        for s in range(X):
            for k in range(2):
                rbuf32[s, k, at_rows, :] = tbuf[:, 2 * s + k, :]

        @pl.when(group == 3)
        def _():
            all_rows = pl.ds(pl.multiple_of(m * 4 * Z, 4 * Z), 4 * Z)
            for s in range(X):
                for k in range(2):
                    obuf[s, k, all_rows, :] = rbuf32[s, k, all_rows, :].astype(BF)
            for d in range(1, X):
                o_copy(d, m).start()

    for copy in started:
        copy.wait_send()
    for d in sorted({HY, 3} if HY > 3 else {HY}):
        for way in range(2):
            for h in y_pieces(way, d - 1):
                if h in y_pieces(way, d):
                    y_copy(way, d, h).wait_send()
                q_copy(Y - d if way == 0 else d, h, c).wait_send()
    ibuf[x] = obuf[x]
    for d in range(1, X):
        for m in range(NM):
            o_copy(d, m).wait_send()
            o_copy(d, m, arrival=True).wait_recv()
    of[...] = ibuf[...].astype(F32).reshape(X * 2 * 8 * 2 * Z, 128)
    for k in range(Z):
        rows = []
        for block in range(X * 2 * 4):
            rows.append(of[pl.ds(block * 4 * Z + (k // GZ) * M + k % GZ, 4, stride=GZ), :])
        rows = jnp.concatenate(rows, axis=0).astype(BF)
        out_ref[:, pl.ds(mod(z + order[k], Z), 1), :] = jnp.dot(
            osel[...], rows, preferred_element_type=F32
        )[:, None, :]


def body(spectra, home, lists, Y, Z):
    dft, sel_s, sel_r, block, band = (jnp.asarray(t) for t in tables())
    vmem = pl.BlockSpec(memory_space=pltpu.VMEM)
    dma = pltpu.SemaphoreType.DMA
    HY = Y // 2
    out = pl.pallas_call(
        functools.partial(kernel, Y, Z),
        out_shape=jax.ShapeDtypeStruct((LIST, Z, LAGS), F32),
        in_specs=[pl.BlockSpec(memory_space=pl.ANY)] * 8,
        out_specs=vmem,
        scratch_shapes=[
            pltpu.VMEM((W, 4, 2 * F), BF),
            pltpu.VMEM((2, 128), jnp.int32),
            pltpu.VMEM((1, LIST), jnp.int32),
            pltpu.VMEM(dft.shape, BF),
            pltpu.VMEM(sel_s.shape, BF),
            pltpu.VMEM(sel_r.shape, F32),
            pltpu.VMEM(block.shape, F32),
            pltpu.VMEM(band.shape, BF),
            pltpu.VMEM((48, 1024), F32),
            pltpu.VMEM((2, 48, 128), F32),
            pltpu.VMEM((2, Y, 2, 48, 512), BF),
            pltpu.VMEM((Z, X, 2, 48, 128), BF),
            pltpu.VMEM((X, 8, 128), F32),
            pltpu.VMEM((Z, W, 16, F), BF),
            pltpu.VMEM((Z, W, 16, F), BF),
            pltpu.VMEM((2 * Y, W, 2, 16, F), BF),
            pltpu.VMEM((Z, 8, 128), F32),
            pltpu.VMEM((X, 2, 16 * Z, 128), F32),
            pltpu.VMEM((X, 2, 16 * Z, 128), BF),
            pltpu.VMEM((X, 2, 16 * Z, 128), BF),
            pltpu.VMEM((128 * Z, 128), F32),
            pltpu.VMEM((128, 128), BF),
            dma((8,)),
            dma((2, HY, 2)), dma((2, HY, 2)),
            dma((Y, 2)), dma((Y, 2)),
            dma((X - 1,)), dma((X - 1,)),
            dma((2,)), dma((2,)),
            dma((Z - 1,)), dma((Z - 1,)),
            dma((X - 1, Z)), dma((X - 1, Z)),
            dma((X - 1, Y // 2)), dma((X - 1, Y // 2)),
        ],
        compiler_params=pltpu.CompilerParams(
            collective_id=0, has_side_effects=True, vmem_limit_bytes=60 * 2**20
        ),
        cost_estimate=pl.CostEstimate(
            flops=6_500_000_000, bytes_accessed=4_000_000, transcendentals=400_000
        ),
    )(spectra.transpose(1, 2, 0, 3)[0], home.reshape(2, 128), lists, dft, sel_s, sel_r, block, band)
    return out[None, :, :, None, :]


def solution(mesh):
    Y = mesh.shape["src"] // (2 * X)
    Z = mesh.shape["rcv"]
    return jax.shard_map(
        functools.partial(body, Y=Y, Z=Z),
        mesh=mesh,
        in_specs=(P("src", "rcv", None, None), P(), P("src", None)),
        out_specs=P("src", None, None, "rcv", None),
        check_vma=False,
    )
```
